256 devices in a mesh: cin: 32 (over y, x, core), cout: 8 (over z).
Axes of the slice: x: 4, y: 4, z: 8, core: 2. Of those that a mesh axis runs over, the one named last changes fastest.
Arguments:
- inputs: bfloat16 [8, 1024, 2048], P('cout', 'cin'), may hold values from -6 to 6
- weight: bfloat16 [27, 1024, 1024], P(None, 'cin', 'cout'), may hold values from -0.0390625 to 0.0390625
- grad_out: bfloat16 [8, 1024, 2048], P(None, 'cout', 'cin'), may hold values from -6 to 6
Outputs:
- output: bfloat16 [8, 1024, 2048], P(None, 'cout', 'cin')
- grad_input: bfloat16 [8, 1024, 2048], P('cout', 'cin')
- grad_weight: float32 [27, 1024, 1024], P(None, 'cin', 'cout')
The draws below stay inside these ranges and needn't reach their ends.
All inputs are finite; a program needn't handle non-finite values.
Results may differ from the reference program's by a relative error of at most 0.0016.
Values may be sent and summed in bfloat16 or wider, within the bound.
No kernel may reach another device: no remote copies, remote signals or barrier semaphores. Data moves between devices by JAX's collectives and lax.ppermute only.
A program may use at most 64 MiB of HBM per device.

```python
import math
import jax
import jax.numpy as jnp
from jax import lax

CIN = 1024
COUT = 1024
SX = 16
SY = 16
SZ = 8
CELLS = 2048
BATCH = 8


def block_levels(rng, extent, split, least, high):
    loudness, own = 1.0, jax.random.fold_in(rng, 6)
    for axis_at, parts in split:
        heights = jnp.exp(jax.random.uniform(jax.random.fold_in(own, axis_at), (parts,), jnp.float32, least / len(split), high / len(split)))
        loudness = loudness * jnp.repeat(heights, extent[axis_at] // parts).reshape([-1 if axis == axis_at else 1 for axis in range(len(extent))])
    return loudness


def bell_draw(own_key, shape, width, most, split=(), kind=jnp.bfloat16):
    values = width * jax.random.normal(own_key, shape, jnp.float32)
    if split:
        values = values * block_levels(own_key, shape, split, -0.22, 0.18)
    return jnp.clip(values, -most, most).astype(kind)


def setup_inputs(seed: int = 0) -> dict:
    key_list = jax.random.split(jax.random.key(seed), 4)
    inputs = bell_draw(key_list[0], (BATCH, CIN, CELLS), 1.0, 6.0, ((0, 8), (1, 32)))
    weight = bell_draw(key_list[1], (27, CIN, COUT), (27 * CIN) ** -0.5, 0.0390625, ((1, 32), (2, 8)))
    grad_out = bell_draw(key_list[2], (BATCH, COUT, CELLS), 1.0, 6.0, ((1, 8), (2, 32)))
    return {"inputs": inputs, "weight": weight, "grad_out": grad_out}


tap_offsets = [(a, b, c) for a in (-1, 0, 1) for b in (-1, 0, 1) for c in (-1, 0, 1)]

def tap_shift(values, a, b, c):
    cell_count = values.shape[-1]
    margin = SY * SZ + SZ + 1
    widths = [(0, 0)] * (values.ndim - 1) + [(margin, margin)]
    padded = jnp.pad(values, widths)
    offset = a * SY * SZ + b * SZ + c
    shifted = lax.slice_in_dim(padded, margin + offset, margin + offset + cell_count, axis=values.ndim - 1)
    position = jnp.arange(cell_count, dtype=jnp.int32)
    coord_x = position // (SY * SZ) + a
    coord_y = position // SZ % SY + b
    coord_z = position % SZ + c
    inside = (coord_x >= 0) & (coord_x < SX) & (coord_y >= 0) & (coord_y < SY) & (coord_z >= 0) & (coord_z < SZ)
    return jnp.where(inside, shifted, jnp.zeros_like(shifted))

def stacked_columns(values, sign):
    return jnp.concatenate([tap_shift(values, sign * a, sign * b, sign * c) for a, b, c in tap_offsets], axis=0)

def reference(inputs, weight, grad_out):
    highest = lax.Precision.HIGHEST
    flat_weight = weight.astype(jnp.float32).reshape(27 * CIN, COUT)
    weight_by_tap = jnp.transpose(weight.astype(jnp.float32), (1, 0, 2)).reshape(CIN, 27 * COUT)

    def one_sample(grad_sum, sample_pair):
        sample, grad_rows = sample_pair
        columns = stacked_columns(sample, 1).astype(jnp.float32)
        out_rows = jnp.dot(flat_weight.T, columns, precision=highest)
        grad_cols = stacked_columns(grad_rows, -1).astype(jnp.float32)
        input_rows = jnp.dot(weight_by_tap, grad_cols, precision=highest)
        grad_sum = grad_sum + jnp.dot(columns, grad_rows.astype(jnp.float32).T, precision=highest)
        return (grad_sum, (out_rows.astype(jnp.bfloat16), input_rows.astype(jnp.bfloat16)))
    grad_sum, (output, grad_input) = lax.scan(one_sample, jnp.zeros((27 * CIN, COUT), jnp.float32), (inputs, grad_out))
    grad_weight = grad_sum.reshape(27, CIN, COUT) / math.sqrt(BATCH * CELLS)
    return (output, grad_input, grad_weight)
```

```python
import functools
import math

import jax
import jax.numpy as jnp
from jax import lax
from jax.experimental import pallas as pl
from jax.experimental.pallas import tpu as pltpu
from jax.sharding import PartitionSpec as P

SX = 16
SY = 16
SZ = 8
PLANE = SY * SZ
SIDE = 4
BF16 = jnp.bfloat16
F16 = jnp.float16
F32 = jnp.float32

in_plane = [(b, c) for b in (-1, 0, 1) for c in (-1, 0, 1)]
VMEM_LIMIT = 40 * 1024 * 1024


def move_xy(value, dy, dx, flip=0):
    pairs = []
    for y in range(SIDE):
        for x in range(SIDE):
            for core in range(2):
                target = ((y + dy) % SIDE * SIDE + (x + dx) % SIDE) * 2 + (core ^ flip)
                pairs.append(((y * SIDE + x) * 2 + core, target))
    return lax.ppermute(value, "cin", pairs)


def swap_cores(value):
    return move_xy(value, 0, 0, 1)


def plane_mask(rows, b, c):
    lane = lax.broadcasted_iota(jnp.int32, (rows, PLANE), 1)
    y = (lane >> 3) + b
    z = (lane & 7) + c
    return (y >= 0) & (y < SY) & (z >= 0) & (z < SZ)


def dgrad_kernel(place, *refs):
    half_a, half_b = refs[0:4], refs[4:8]
    wd_ref, taps_ref, out_ref = refs[8:11]
    ci = out_ref.shape[1]
    co = taps_ref.shape[2] // 3
    n = pl.program_id(0)
    my_y, my_x = place[0], place[1]

    def fill(parts, first, second, flip):
        for p in range(SX):
            y, x = p // SIDE, p % SIDE
            rel_y = lax.rem(my_y - y + SIDE, SIDE)
            rel_x = lax.rem(my_x - x + SIDE, SIDE)
            outer, inner = (rel_y, rel_x) if not flip else (rel_x, rel_y)
            for index in range(4):

                @pl.when(outer == index)
                def _():
                    cells = parts[index][inner, lax.rem(n, 2)]
                    for a in (-1, 0, 1):
                        q = p + a
                        if 0 <= q < SX:
                            taps_ref[0, q * PLANE : (q + 1) * PLANE, (a + 1) * co : (a + 2) * co] = cells

    taps_ref[0, (SX - 1) * PLANE :, 0:co] = jnp.zeros((PLANE, co), BF16)
    taps_ref[0, 0:PLANE, 2 * co :] = jnp.zeros((PLANE, co), BF16)

    @pl.when(n < 2)
    def _():
        fill(half_a, 0, 1, False)

    @pl.when(n >= 2)
    def _():
        fill(half_b, 0, 1, True)

    wd = wd_ref[...]
    step = 4
    for first in range(0, SX, step):
        rows = taps_ref[0, first * PLANE : (first + step) * PLANE, :]
        product = lax.dot_general(wd, rows, (((1,), (1,)), ((), ())), preferred_element_type=F32)
        for j in range(step):
            total = None
            for index, (b, c) in enumerate(in_plane):
                term = product[index * ci : (index + 1) * ci, j * PLANE : (j + 1) * PLANE]
                shift = (b * SZ + c) % PLANE
                if shift:
                    term = jnp.where(plane_mask(ci, -b, -c), pltpu.roll(term, shift, 1), 0.0)
                total = term if total is None else total + term
            out_ref[0, :, (first + j) * PLANE : (first + j + 1) * PLANE] = total


def fwd_kernel(place, in_ref, wa_ref, cols_ref, out_a, out_b, peak_ref, stage):
    ci = in_ref.shape[1]
    co = wa_ref.shape[0] // 3
    n = pl.program_id(0)
    my_y, my_x = place[0], place[1]

    @pl.when(n == 0)
    def _():
        peak_ref[...] = jnp.zeros_like(peak_ref)

    for p in range(SX):
        cells = in_ref[0, :, p * PLANE : (p + 1) * PLANE].astype(F32)
        for index, (b, c) in enumerate(in_plane):
            shift = -(b * SZ + c) % PLANE
            term = cells
            if shift:
                term = jnp.where(plane_mask(ci, b, c), pltpu.roll(term, shift, 1), 0.0)
            cols_ref[0, index * ci : (index + 1) * ci, p * PLANE : (p + 1) * PLANE] = term.astype(BF16)

    step = 4
    for first in range(0, SX, step):
        lanes = slice(first * PLANE, (first + step) * PLANE)
        stage[:, lanes] = jnp.dot(wa_ref[...], cols_ref[0, :, lanes], preferred_element_type=F32)

    peak = None
    for p in range(SX):
        total = stage[co : 2 * co, p * PLANE : (p + 1) * PLANE]
        if p > 0:
            total = total + stage[0:co, (p - 1) * PLANE : p * PLANE]
        if p < SX - 1:
            total = total + stage[2 * co :, (p + 1) * PLANE : (p + 2) * PLANE]
        y, x = p // SIDE, p % SIDE
        rel_y = lax.rem(y - my_y + SIDE, SIDE)
        rel_x = lax.rem(x - my_x + SIDE, SIDE)

        @pl.when(n < 2)
        def _():
            out_a[rel_x, rel_y, lax.rem(n, 2)] = total

        @pl.when(n >= 2)
        def _():
            out_b[rel_y, rel_x, lax.rem(n, 2)] = total

        size = jnp.abs(total)
        peak = size if peak is None else jnp.maximum(peak, size)
    peak_ref[...] = jnp.maximum(peak_ref[...], peak)


def wgrad_kernel(cols_ref, taps_ref, out_ref):
    @pl.when(pl.program_id(0) == 0)
    def _():
        out_ref[...] = jnp.zeros_like(out_ref)

    out_ref[...] += jnp.dot(cols_ref[0], taps_ref[0], preferred_element_type=F32)


def whole(shape):
    return pl.BlockSpec(shape, lambda *_: (0,) * len(shape))


def per_sample(shape):
    return pl.BlockSpec((1,) + shape, lambda n, *_: (n,) + (0,) * len(shape))


def coded(block, power):
    rows = (block * jnp.exp2(power)).reshape(-1, block.shape[-1]).astype(F16)
    note = jnp.broadcast_to(power, (16, block.shape[-1])).astype(F16)
    return jnp.concatenate([rows, note], axis=0)


def decoded(message, shape):
    power = message[-1, 0].astype(F32)
    return message[:-16].astype(F32).reshape(shape) * jnp.exp2(-power), power


def reduce_stage(blocks, power, moves):
    arrived = [moves[s](coded(blocks[s], power)) for s in (1, 2, 3)]
    total, least = blocks[0], power
    for message in arrived:
        value, other = decoded(message, total.shape)
        total, least = total + value, jnp.minimum(least, other)
    return total, least


def body(inputs, weight, grad_out):
    ci, co = weight.shape[1], weight.shape[2]
    where_cin = lax.axis_index("cin")
    core = where_cin % 2
    place = jnp.stack([where_cin // 2 // SIDE, where_cin // 2 % SIDE]).astype(jnp.int32)
    batch = grad_out.shape[0]
    mine = batch // 2
    first_core = core == 0

    def split(value, size, axis):
        own = lax.dynamic_slice_in_dim(value, core * size, size, axis)
        other = lax.dynamic_slice_in_dim(value, (1 - core) * size, size, axis)
        return own, other

    def in_order(own, other, axis):
        return jnp.where(
            first_core,
            jnp.concatenate([own, other], axis),
            jnp.concatenate([other, own], axis),
        )

    gathered = lax.all_gather(inputs, "cout", axis=0, tiled=True)

    own, other = split(jnp.transpose(grad_out, (0, 2, 1)), mine, 0)
    plane = in_order(own, swap_cores(other), 1)
    along_x = [None] + [functools.partial(move_xy, dy=0, dx=s) for s in (1, 2, 3)]
    along_y = [None] + [functools.partial(move_xy, dy=s, dx=0) for s in (1, 2, 3)]

    def gather_stage(value, moves):
        return [value] + [moves[s](value) for s in (1, 2, 3)]

    row_a = jnp.stack(gather_stage(plane[: mine // 2], along_x))
    row_b = jnp.stack(gather_stage(plane[mine // 2 :], along_y))
    parts = gather_stage(row_a, along_y) + gather_stage(row_b, along_x)

    pair = in_order(weight, swap_cores(weight), 1)
    wd = jnp.transpose(pair.reshape(3, 9, 2 * ci, co), (1, 2, 0, 3)).reshape(9 * 2 * ci, 3 * co)
    wa = wd.T

    cells = inputs.shape[2]
    params = pltpu.CompilerParams(vmem_limit_bytes=VMEM_LIMIT)
    taps, input_term = pl.pallas_call(
        dgrad_kernel,
        grid_spec=pltpu.PrefetchScalarGridSpec(
            num_scalar_prefetch=1,
            grid=(mine,),
            in_specs=[whole(p.shape) for p in parts] + [whole(wd.shape)],
            out_specs=[per_sample((cells, 3 * co)), per_sample((2 * ci, cells))],
        ),
        out_shape=[
            jax.ShapeDtypeStruct((mine, cells, 3 * co), BF16),
            jax.ShapeDtypeStruct((mine, 2 * ci, cells), F32),
        ],
        compiler_params=params,
        name="dgrad",
    )(place, *parts, wd)

    own, other = split(input_term, ci, 1)
    input_term = in_order(own, swap_cores(other), 0)
    grad_input = lax.psum_scatter(input_term, "cout", scatter_dimension=0, tiled=True).astype(BF16)

    own, other = split(gathered, mine, 0)
    sample = in_order(own, swap_cores(other), 1)
    half = (SIDE, SIDE, mine // 2, co, PLANE)
    columns, out_a, out_b, peak = pl.pallas_call(
        fwd_kernel,
        grid_spec=pltpu.PrefetchScalarGridSpec(
            num_scalar_prefetch=1,
            grid=(mine,),
            in_specs=[per_sample((2 * ci, cells)), whole(wa.shape)],
            out_specs=[per_sample((9 * 2 * ci, cells)), whole(half), whole(half), whole((co, PLANE))],
            scratch_shapes=[pltpu.VMEM((3 * co, cells), F32)],
        ),
        out_shape=[
            jax.ShapeDtypeStruct((mine, 9 * 2 * ci, cells), BF16),
            jax.ShapeDtypeStruct(half, F32),
            jax.ShapeDtypeStruct(half, F32),
            jax.ShapeDtypeStruct((co, PLANE), F32),
        ],
        compiler_params=params,
        name="forward",
    )(place, sample, wa)

    power = 14.0 - jnp.ceil(jnp.log2(jnp.maximum(jnp.max(peak), 1e-30)))
    sum_a, power_a = reduce_stage(out_a, power, along_x)
    sum_b, power_b = reduce_stage(out_b, power, along_y)
    sum_a, _ = reduce_stage(sum_a, power_a - 2.0, along_y)
    sum_b, _ = reduce_stage(sum_b, power_b - 2.0, along_x)
    output = jnp.transpose(jnp.concatenate([sum_a, sum_b], 0).astype(BF16), (0, 2, 1))
    own, other = split(output, PLANE // 2, 1)
    output = jnp.transpose(in_order(own, swap_cores(other), 0), (0, 2, 1))

    grad_sum = pl.pallas_call(
        wgrad_kernel,
        grid=(mine,),
        in_specs=[per_sample((9 * 2 * ci, cells)), per_sample((cells, 3 * co))],
        out_specs=whole((9 * 2 * ci, 3 * co)),
        out_shape=jax.ShapeDtypeStruct((9 * 2 * ci, 3 * co), F32),
        compiler_params=params,
        name="wgrad",
    )(columns, taps)
    grad_sum = jnp.transpose(grad_sum.reshape(9, 2 * ci, 3, co), (2, 0, 1, 3)).reshape(27, 2 * ci, co)
    own, other = split(grad_sum, ci, 1)
    grad_weight = (own + swap_cores(other)) / math.sqrt(batch * cells)
    return output, grad_input, grad_weight


def solution(mesh):
    placed = (P("cout", "cin", None), P(None, "cin", "cout"), P(None, "cout", "cin"))
    return jax.shard_map(
        body,
        mesh=mesh,
        in_specs=placed,
        out_specs=(P(None, "cout", "cin"), P("cout", "cin", None), P(None, "cin", "cout")),
        check_vma=False,
    )
```

```python
import functools
import math

import jax
import jax.numpy as jnp
from jax import lax
from jax.experimental import pallas as pl
from jax.experimental.pallas import tpu as pltpu
from jax.sharding import PartitionSpec as P

SX = 16
SY = 16
SZ = 8
PLANE = SY * SZ
SIDE = 4
BF16 = jnp.bfloat16
F16 = jnp.float16
F32 = jnp.float32

in_plane = [(b, c) for b in (-1, 0, 1) for c in (-1, 0, 1)]
VMEM_LIMIT = 24 * 1024 * 1024
NOTE = 16
TINY = 1e-32


def move_xy(value, dy, dx, flip=0):
    pairs = []
    for y in range(SIDE):
        for x in range(SIDE):
            for core in range(2):
                target = ((y + dy) % SIDE * SIDE + (x + dx) % SIDE) * 2 + (core ^ flip)
                pairs.append(((y * SIDE + x) * 2 + core, target))
    return lax.ppermute(value, "cin", pairs)


def swap_cores(value):
    return move_xy(value, 0, 0, 1)


def plane_mask(rows, b, c):
    lane = lax.broadcasted_iota(jnp.int32, (rows, PLANE), 1)
    y = (lane >> 3) + b
    z = (lane & 7) + c
    return (y >= 0) & (y < SY) & (z >= 0) & (z < SZ)


def dgrad_kernel(place, *refs):
    half_a, half_b = refs[0:4], refs[4:8]
    wd_ref, taps_ref, own_ref, other_ref = refs[8:12]
    ci = own_ref.shape[1]
    co = taps_ref.shape[2] // 3
    n = pl.program_id(0)
    my_y, my_x, core = place[0], place[1], place[2]

    def fill(parts, y_first):
        for first in range(SIDE):
            for second in range(SIDE):
                step_y, step_x = (first, second) if y_first else (second, first)
                y = lax.rem(my_y - step_y + SIDE, SIDE)
                x = lax.rem(my_x - step_x + SIDE, SIDE)
                p = y * SIDE + x
                cells = parts[first][second, lax.rem(n, 2)]

                def put(q, column):
                    row = pl.multiple_of(q * PLANE, PLANE)
                    taps_ref[0, pl.ds(row, PLANE), column * co : (column + 1) * co] = cells

                put(p, 1)
                pl.when(p > 0)(lambda: put(p - 1, 0))
                pl.when(p < SX - 1)(lambda: put(p + 1, 2))

    taps_ref[0, (SX - 1) * PLANE :, 0:co] = jnp.zeros((PLANE, co), BF16)
    taps_ref[0, 0:PLANE, 2 * co :] = jnp.zeros((PLANE, co), BF16)
    pl.when(n < 2)(lambda: fill(half_a, True))
    pl.when(n >= 2)(lambda: fill(half_b, False))

    wd = wd_ref[...]
    masks = [plane_mask(2 * ci, -b, -c) for b, c in in_plane]
    step = 4
    for first in range(0, SX, step):
        rows = taps_ref[0, first * PLANE : (first + step) * PLANE, :]
        product = lax.dot_general(wd, rows, (((1,), (1,)), ((), ())), preferred_element_type=F32)
        for j in range(step):
            total = None
            for index, (b, c) in enumerate(in_plane):
                term = product[index * 2 * ci : (index + 1) * 2 * ci, j * PLANE : (j + 1) * PLANE]
                shift = (b * SZ + c) % PLANE
                if shift:
                    term = jnp.where(masks[index], pltpu.roll(term, shift, 1), 0.0)
                total = term if total is None else total + term
            lanes = slice((first + j) * PLANE, (first + j + 1) * PLANE)
            low, high = total[:ci], total[ci:]
            own_ref[0, :, lanes] = jnp.where(core == 0, low, high)
            other_ref[0, :, lanes] = jnp.where(core == 0, high, low)


def fwd_kernel(place, own_ref, other_ref, wa_ref, cols_ref, msg_a, msg_b, own_a, own_b, stage, sums):
    ci = own_ref.shape[1]
    co = wa_ref.shape[0] // 3
    n = pl.program_id(0)
    my_y, my_x, core = place[0], place[1], place[2]
    masks = [plane_mask(2 * ci, b, c) for b, c in in_plane]

    @pl.when(n == 0)
    def _():
        stage[0] = jnp.zeros(stage.shape[1:], F32)
        stage[SX + 1] = jnp.zeros(stage.shape[1:], F32)

    for p in range(SX):
        lanes = slice(p * PLANE, (p + 1) * PLANE)
        mine = own_ref[0, :, lanes].astype(F32)
        got = other_ref[0, :, lanes].astype(F32)
        cells = jnp.concatenate([jnp.where(core == 0, mine, got), jnp.where(core == 0, got, mine)], axis=0)
        for index, (b, c) in enumerate(in_plane):
            shift = -(b * SZ + c) % PLANE
            term = cells
            if shift:
                term = jnp.where(masks[index], pltpu.roll(term, shift, 1), 0.0)
            cols_ref[0, index * 2 * ci : (index + 1) * 2 * ci, lanes] = term.astype(BF16)

    step = 4
    for first in range(0, SX, step):
        lanes = slice(first * PLANE, (first + step) * PLANE)
        product = jnp.dot(wa_ref[...], cols_ref[0, :, lanes], preferred_element_type=F32)
        for j in range(step):
            stage[first + j + 1] = product[:, j * PLANE : (j + 1) * PLANE]

    peak = jnp.zeros((co, PLANE), F32)
    for p in range(SX):
        total = stage[p, 0:co] + stage[p + 1, co : 2 * co] + stage[p + 2, 2 * co :]
        sums[p] = total
        peak = jnp.maximum(peak, jnp.abs(total))
    peak = jnp.full((NOTE, PLANE), jnp.maximum(jnp.max(peak), TINY), F32)
    power = 14.0 - jnp.ceil(jnp.log2(peak))
    factor = jnp.exp2(power[0:1])
    rows = SIDE * co
    at = lax.rem(n, 2)

    def send(msg, own, y_first):
        for first in range(SIDE):
            if first == 0:
                own[at, rows:] = power
            else:
                msg[first - 1, at, rows:] = power
            for second in range(SIDE):
                step_y, step_x = (first, second) if y_first else (second, first)
                y = lax.rem(my_y + step_y, SIDE)
                x = lax.rem(my_x + step_x, SIDE)
                total = sums[y * SIDE + x]
                if first == 0:
                    own[at, second * co : (second + 1) * co] = total
                else:
                    msg[first - 1, at, second * co : (second + 1) * co] = total * factor

    pl.when(n < 2)(lambda: send(msg_a, own_a, False))
    pl.when(n >= 2)(lambda: send(msg_b, own_b, True))


def arrived(own, messages, rows):
    total, least = own[:, :rows], own[:, rows:]
    for message in messages:
        power = message[:, rows:]
        total = total + message[:, :rows] * jnp.exp2(-power[:, 0:1])
        least = jnp.minimum(least, power)
    return total, least


def turn_kernel(*refs):
    ins, outs = refs[:8], refs[8:]
    for half in range(2):
        own, messages = ins[4 * half], ins[4 * half + 1 : 4 * half + 4]
        msg, mine = outs[2 * half : 2 * half + 2]
        rows = own.shape[1] - NOTE
        size = rows // SIDE
        total, least = arrived(own[...], [m[...] for m in messages], rows)
        power = least - 2.0
        mine[:, :size] = total[:, :size]
        mine[:, size:] = power
        for step in range(1, SIDE):
            msg[step - 1, :, :size] = total[:, step * size : (step + 1) * size] * jnp.exp2(power[:, 0:1])
            msg[step - 1, :, size:] = power


def last_kernel(place, *refs):
    ins, own_ref, other_ref = refs[:8], refs[8], refs[9]
    part = PLANE // 2
    for half in range(2):
        own, messages = ins[4 * half], ins[4 * half + 1 : 4 * half + 4]
        rows = own.shape[1] - NOTE
        total, _ = arrived(own[...], [m[...] for m in messages], rows)
        for at in range(total.shape[0]):
            cells = total[at].T.astype(BF16)
            low, high = cells[:part], cells[part:]
            own_ref[half * total.shape[0] + at] = jnp.where(place[2] == 0, low, high)
            other_ref[half * total.shape[0] + at] = jnp.where(place[2] == 0, high, low)


def wgrad_kernel(place, cols_ref, taps_ref, own_ref, other_ref, acc):
    ci, co = own_ref.shape[1:]
    n = pl.program_id(0)

    @pl.when(n == 0)
    def _():
        acc[...] = jnp.zeros_like(acc)

    acc[...] += jnp.dot(cols_ref[0], taps_ref[0], preferred_element_type=F32)

    @pl.when(n == pl.num_programs(0) - 1)
    def _():
        for tap in range(27):
            first, column = tap % 9 * 2 * ci, tap // 9 * co
            low = acc[first : first + ci, column : column + co]
            high = acc[first + ci : first + 2 * ci, column : column + co]
            own_ref[tap] = jnp.where(place[2] == 0, low, high)
            other_ref[tap] = jnp.where(place[2] == 0, high, low)


def whole(shape):
    return pl.BlockSpec(shape, lambda *_: (0,) * len(shape))


def per_sample(shape):
    return pl.BlockSpec((1,) + shape, lambda n, *_: (n,) + (0,) * len(shape))


def body(inputs, weight, grad_out):
    ci, co = weight.shape[1], weight.shape[2]
    where_cin = lax.axis_index("cin")
    core = where_cin % 2
    place = jnp.stack([where_cin // 2 // SIDE, where_cin // 2 % SIDE, core]).astype(jnp.int32)
    batch = grad_out.shape[0]
    mine = batch // 2
    pairs = mine // 2
    first_core = core == 0

    def taken(value, which, size, axis):
        return lax.dynamic_slice_in_dim(value, which * size, size, axis)

    def in_order(own, other, axis):
        return jnp.where(
            first_core,
            jnp.concatenate([own, other], axis),
            jnp.concatenate([other, own], axis),
        )

    gathered = lax.all_gather(inputs, "cout", axis=0, tiled=True)

    cotangent = jnp.transpose(grad_out, (0, 2, 1))
    got = swap_cores(taken(cotangent, 1 - core, mine, 0))
    plane = in_order(taken(cotangent, core, mine, 0), got, 1)
    along_x = [functools.partial(move_xy, dy=0, dx=s) for s in (1, 2, 3)]
    along_y = [functools.partial(move_xy, dy=s, dx=0) for s in (1, 2, 3)]

    def gather_stage(value, moves):
        return [value] + [move(value) for move in moves]

    near_a, near_b = lax.optimization_barrier(
        (gather_stage(plane[:pairs], along_x), gather_stage(plane[pairs:], along_y))
    )
    row_a, row_b = lax.optimization_barrier((jnp.stack(near_a), jnp.stack(near_b)))
    parts = gather_stage(row_a, along_y) + gather_stage(row_b, along_x)

    sample = swap_cores(taken(gathered, 1 - core, mine, 0))

    pair = in_order(weight, swap_cores(weight), 1)
    wd = jnp.transpose(pair.reshape(3, 9, 2 * ci, co), (1, 2, 0, 3)).reshape(9 * 2 * ci, 3 * co)
    wa = wd.T

    cells = inputs.shape[2]
    params = pltpu.CompilerParams(vmem_limit_bytes=VMEM_LIMIT)
    taps, terms, other = pl.pallas_call(
        dgrad_kernel,
        grid_spec=pltpu.PrefetchScalarGridSpec(
            num_scalar_prefetch=1,
            grid=(mine,),
            in_specs=[whole(p.shape) for p in parts] + [whole(wd.shape)],
            out_specs=[
                per_sample((cells, 3 * co)),
                pl.BlockSpec((1, ci, cells), lambda n, place: (place[2] * mine + n, 0, 0)),
                per_sample((ci, cells)),
            ],
        ),
        out_shape=[
            pltpu.HBM((mine, cells, 3 * co), BF16),
            pltpu.HBM((batch, ci, cells), F32),
            pltpu.HBM((mine, ci, cells), F32),
        ],
        compiler_params=params,
        name="dgrad",
    )(place, *parts, wd)
    taps = pltpu.with_memory_space_constraint(taps, pltpu.HBM)

    terms = lax.dynamic_update_slice_in_dim(terms, swap_cores(other), (1 - core) * mine, 0)
    grad_input = lax.psum_scatter(terms, "cout", scatter_dimension=0, tiled=True).astype(BF16)

    rows = SIDE * co + NOTE
    sent = jax.ShapeDtypeStruct((SIDE - 1, pairs, rows, PLANE), F32)
    kept = jax.ShapeDtypeStruct((pairs, rows, PLANE), F32)
    columns, msg_a, msg_b, own_a, own_b = pl.pallas_call(
        fwd_kernel,
        grid_spec=pltpu.PrefetchScalarGridSpec(
            num_scalar_prefetch=1,
            grid=(mine,),
            in_specs=[
                pl.BlockSpec((1, ci, cells), lambda n, place: (place[2] * mine + n, 0, 0)),
                per_sample((ci, cells)),
                whole(wa.shape),
            ],
            out_specs=[per_sample((9 * 2 * ci, cells))] + [whole(o.shape) for o in (sent, sent, kept, kept)],
            scratch_shapes=[pltpu.VMEM((SX + 2, 3 * co, PLANE), F32), pltpu.VMEM((SX, co, PLANE), F32)],
        ),
        out_shape=[pltpu.HBM((mine, 9 * 2 * ci, cells), BF16), sent, sent, kept, kept],
        compiler_params=params,
        name="forward",
    )(place, gathered, sample, wa)
    columns = pltpu.with_memory_space_constraint(columns, pltpu.HBM)

    def reduce_stage(msg, moves):
        return [move(msg[i].astype(F16)).astype(F32) for i, move in enumerate(moves)]

    rows = co + NOTE
    sent = jax.ShapeDtypeStruct((SIDE - 1, pairs, rows, PLANE), F32)
    kept = jax.ShapeDtypeStruct((pairs, rows, PLANE), F32)
    msg_a, own_a, msg_b, own_b = pl.pallas_call(
        turn_kernel, out_shape=[sent, kept, sent, kept], compiler_params=params, name="turn"
    )(own_a, *reduce_stage(msg_a, along_x), own_b, *reduce_stage(msg_b, along_y))
    ends = [own_a, *reduce_stage(msg_a, along_y), own_b, *reduce_stage(msg_b, along_x)]
    own, other = pl.pallas_call(
        last_kernel,
        grid_spec=pltpu.PrefetchScalarGridSpec(
            num_scalar_prefetch=1,
            grid=(1,),
            in_specs=[whole(e.shape) for e in ends],
            out_specs=[whole((mine, PLANE // 2, co))] * 2,
        ),
        out_shape=[jax.ShapeDtypeStruct((mine, PLANE // 2, co), BF16)] * 2,
        compiler_params=params,
        name="last",
    )(place, *ends)
    output = jnp.transpose(in_order(own, swap_cores(other), 0), (0, 2, 1))

    own, other = pl.pallas_call(
        wgrad_kernel,
        grid_spec=pltpu.PrefetchScalarGridSpec(
            num_scalar_prefetch=1,
            grid=(mine,),
            in_specs=[per_sample((9 * 2 * ci, cells)), per_sample((cells, 3 * co))],
            out_specs=[whole((27, ci, co))] * 2,
            scratch_shapes=[pltpu.VMEM((9 * 2 * ci, 3 * co), F32)],
        ),
        out_shape=[jax.ShapeDtypeStruct((27, ci, co), F32)] * 2,
        compiler_params=params,
        name="wgrad",
    )(place, columns, taps)
    grad_weight = (own + swap_cores(other)) / math.sqrt(batch * cells)
    return output, grad_input, grad_weight


def solution(mesh):
    placed = (P("cout", "cin", None), P(None, "cin", "cout"), P(None, "cout", "cin"))
    return jax.shard_map(
        body,
        mesh=mesh,
        in_specs=placed,
        out_specs=(P(None, "cout", "cin"), P("cout", "cin", None), P(None, "cin", "cout")),
        check_vma=False,
    )
```

```python
import functools
import math

import jax
import jax.numpy as jnp
from jax import lax
from jax.experimental import pallas as pl
from jax.experimental.pallas import tpu as pltpu
from jax.sharding import PartitionSpec as P

SX = 16
SY = 16
SZ = 8
PLANE = SY * SZ
SIDE = 4
BF16 = jnp.bfloat16
F16 = jnp.float16
F32 = jnp.float32

in_plane = [(b, c) for b in (-1, 0, 1) for c in (-1, 0, 1)]
VMEM_LIMIT = 24 * 1024 * 1024
NOTE = 16
TINY = 1e-32


def move_xy(value, dy, dx, flip=0):
    pairs = []
    for y in range(SIDE):
        for x in range(SIDE):
            for core in range(2):
                target = ((y + dy) % SIDE * SIDE + (x + dx) % SIDE) * 2 + (core ^ flip)
                pairs.append(((y * SIDE + x) * 2 + core, target))
    return lax.ppermute(value, "cin", pairs)


def swap_cores(value):
    return move_xy(value, 0, 0, 1)


def plane_mask(rows, b, c):
    lane = lax.broadcasted_iota(jnp.int32, (rows, PLANE), 1)
    y = (lane >> 3) + b
    z = (lane & 7) + c
    return (y >= 0) & (y < SY) & (z >= 0) & (z < SZ)


def dgrad_kernel(half, place, *refs):
    parts, wd_ref = refs[:SIDE], refs[SIDE]
    taps_ref, own_ref, other_ref = refs[-3:]
    ci = own_ref.shape[1]
    co = taps_ref.shape[2] // 3
    n = pl.program_id(0)
    my_y, my_x, core = place[0], place[1], place[2]

    def fill(y_first):
        for first in range(SIDE):
            for second in range(SIDE):
                step_y, step_x = (first, second) if y_first else (second, first)
                y = lax.rem(my_y - step_y + SIDE, SIDE)
                x = lax.rem(my_x - step_x + SIDE, SIDE)
                p = y * SIDE + x
                cells = parts[first][second, n]

                def put(q, column):
                    row = pl.multiple_of(q * PLANE, PLANE)
                    taps_ref[0, pl.ds(row, PLANE), column * co : (column + 1) * co] = cells

                put(p, 1)
                pl.when(p > 0)(lambda: put(p - 1, 0))
                pl.when(p < SX - 1)(lambda: put(p + 1, 2))

    taps_ref[0, (SX - 1) * PLANE :, 0:co] = jnp.zeros((PLANE, co), BF16)
    taps_ref[0, 0:PLANE, 2 * co :] = jnp.zeros((PLANE, co), BF16)
    fill(half == 0)

    wd = wd_ref[...]
    masks = [plane_mask(2 * ci, -b, -c) for b, c in in_plane]
    step = 4
    for first in range(0, SX, step):
        rows = taps_ref[0, first * PLANE : (first + step) * PLANE, :]
        product = lax.dot_general(wd, rows, (((1,), (1,)), ((), ())), preferred_element_type=F32)
        for j in range(step):
            total = None
            for index, (b, c) in enumerate(in_plane):
                term = product[index * 2 * ci : (index + 1) * 2 * ci, j * PLANE : (j + 1) * PLANE]
                shift = (b * SZ + c) % PLANE
                if shift:
                    term = jnp.where(masks[index], pltpu.roll(term, shift, 1), 0.0)
                total = term if total is None else total + term
            lanes = slice((first + j) * PLANE, (first + j + 1) * PLANE)
            low, high = total[:ci], total[ci:]
            own_ref[0, :, lanes] = jnp.where(core == 0, low, high)
            other_ref[0, :, lanes] = jnp.where(core == 0, high, low)


def fwd_kernel(half, place, own_ref, other_ref, wa_ref, cols_ref, msg, own, stage, sums):
    ci = own_ref.shape[1]
    co = wa_ref.shape[0] // 3
    n = pl.program_id(0)
    my_y, my_x, core = place[0], place[1], place[2]
    masks = [plane_mask(2 * ci, b, c) for b, c in in_plane]

    @pl.when(n == 0)
    def _():
        stage[0] = jnp.zeros(stage.shape[1:], F32)
        stage[SX + 1] = jnp.zeros(stage.shape[1:], F32)

    for p in range(SX):
        lanes = slice(p * PLANE, (p + 1) * PLANE)
        mine = own_ref[0, :, lanes].astype(F32)
        got = other_ref[0, :, lanes].astype(F32)
        cells = jnp.concatenate([jnp.where(core == 0, mine, got), jnp.where(core == 0, got, mine)], axis=0)
        for index, (b, c) in enumerate(in_plane):
            shift = -(b * SZ + c) % PLANE
            term = cells
            if shift:
                term = jnp.where(masks[index], pltpu.roll(term, shift, 1), 0.0)
            cols_ref[n, index * 2 * ci : (index + 1) * 2 * ci, lanes] = term.astype(BF16)

    step = 4
    for first in range(0, SX, step):
        lanes = slice(first * PLANE, (first + step) * PLANE)
        product = jnp.dot(wa_ref[...], cols_ref[n, :, lanes], preferred_element_type=F32)
        for j in range(step):
            stage[first + j + 1] = product[:, j * PLANE : (j + 1) * PLANE]

    peak = jnp.zeros((co, PLANE), F32)
    for p in range(SX):
        total = stage[p, 0:co] + stage[p + 1, co : 2 * co] + stage[p + 2, 2 * co :]
        sums[p] = total
        peak = jnp.maximum(peak, jnp.abs(total))
    peak = jnp.full((NOTE, PLANE), jnp.maximum(jnp.max(peak), TINY), F32)
    power = 14.0 - jnp.ceil(jnp.log2(peak))
    factor = jnp.exp2(power[0:1])
    rows = SIDE * co

    def send(y_first):
        for first in range(SIDE):
            if first == 0:
                own[n, rows:] = power
            else:
                msg[first - 1, n, rows:] = power
            for second in range(SIDE):
                step_y, step_x = (first, second) if y_first else (second, first)
                y = lax.rem(my_y + step_y, SIDE)
                x = lax.rem(my_x + step_x, SIDE)
                total = sums[y * SIDE + x]
                if first == 0:
                    own[n, second * co : (second + 1) * co] = total
                else:
                    msg[first - 1, n, second * co : (second + 1) * co] = total * factor

    send(half == 1)


def arrived(own, messages, rows):
    total, least = own[:, :rows], own[:, rows:]
    for message in messages:
        power = message[:, rows:]
        total = total + message[:, :rows] * jnp.exp2(-power[:, 0:1])
        least = jnp.minimum(least, power)
    return total, least


def turn_kernel(own, one, two, three, msg, mine):
    rows = own.shape[1] - NOTE
    size = rows // SIDE
    total, least = arrived(own[...], [one[...], two[...], three[...]], rows)
    power = least - 2.0
    mine[:, :size] = total[:, :size]
    mine[:, size:] = power
    for step in range(1, SIDE):
        msg[step - 1, :, :size] = total[:, step * size : (step + 1) * size] * jnp.exp2(power[:, 0:1])
        msg[step - 1, :, size:] = power


def last_kernel(place, *refs):
    ins, own_ref, other_ref = refs[:8], refs[8], refs[9]
    part = PLANE // 2
    for half in range(2):
        own, messages = ins[4 * half], ins[4 * half + 1 : 4 * half + 4]
        rows = own.shape[1] - NOTE
        total, _ = arrived(own[...], [m[...] for m in messages], rows)
        for at in range(total.shape[0]):
            cells = total[at].T.astype(BF16)
            low, high = cells[:part], cells[part:]
            own_ref[half * total.shape[0] + at] = jnp.where(place[2] == 0, low, high)
            other_ref[half * total.shape[0] + at] = jnp.where(place[2] == 0, high, low)


def wgrad_kernel(place, cols_a, cols_b, taps_a, taps_b, own_ref, other_ref, acc):
    ci, co = own_ref.shape[1:]
    n = pl.program_id(0)

    @pl.when(n == 0)
    def _():
        acc[...] = jnp.zeros_like(acc)

    acc[...] += jnp.dot(cols_a[n], taps_a[0], preferred_element_type=F32)
    acc[...] += jnp.dot(cols_b[n], taps_b[0], preferred_element_type=F32)

    @pl.when(n == pl.num_programs(0) - 1)
    def _():
        for tap in range(27):
            first, column = tap % 9 * 2 * ci, tap // 9 * co
            low = acc[first : first + ci, column : column + co]
            high = acc[first + ci : first + 2 * ci, column : column + co]
            own_ref[tap] = jnp.where(place[2] == 0, low, high)
            other_ref[tap] = jnp.where(place[2] == 0, high, low)


def whole(shape):
    return pl.BlockSpec(shape, lambda *_: (0,) * len(shape))


def per_sample(shape):
    return pl.BlockSpec((1,) + shape, lambda n, *_: (n,) + (0,) * len(shape))


def body(inputs, weight, grad_out):
    ci, co = weight.shape[1], weight.shape[2]
    where_cin = lax.axis_index("cin")
    core = where_cin % 2
    place = jnp.stack([where_cin // 2 // SIDE, where_cin // 2 % SIDE, core]).astype(jnp.int32)
    batch = grad_out.shape[0]
    mine = batch // 2
    pairs = mine // 2
    first_core = core == 0

    def taken(value, which, size, axis):
        return lax.dynamic_slice_in_dim(value, which * size, size, axis)

    def in_order(own, other, axis):
        return jnp.where(
            first_core,
            jnp.concatenate([own, other], axis),
            jnp.concatenate([other, own], axis),
        )

    gathered = lax.all_gather(inputs, "cout", axis=0, tiled=True)

    cotangent = jnp.transpose(grad_out, (0, 2, 1))
    got = swap_cores(taken(cotangent, 1 - core, mine, 0))
    plane = in_order(taken(cotangent, core, mine, 0), got, 1)
    along_x = [functools.partial(move_xy, dy=0, dx=s) for s in (1, 2, 3)]
    along_y = [functools.partial(move_xy, dy=s, dx=0) for s in (1, 2, 3)]

    def gather_stage(value, moves):
        return [value] + [move(value) for move in moves]

    near_a, near_b = lax.optimization_barrier(
        (gather_stage(plane[:pairs], along_x), gather_stage(plane[pairs:], along_y))
    )
    row_a, row_b = lax.optimization_barrier((jnp.stack(near_a), jnp.stack(near_b)))
    parts = gather_stage(row_a, along_y), gather_stage(row_b, along_x)

    pair = in_order(weight, swap_cores(weight), 1)
    wd = jnp.transpose(pair.reshape(3, 9, 2 * ci, co), (1, 2, 0, 3)).reshape(9 * 2 * ci, 3 * co)
    wa = wd.T

    cells = inputs.shape[2]
    params = pltpu.CompilerParams(vmem_limit_bytes=VMEM_LIMIT)
    def dgrad(half, earlier):
        place_of = lambda n, place: (place[2] * mine + half * pairs + n, 0, 0)
        taps, terms, other = pl.pallas_call(
            functools.partial(dgrad_kernel, half),
            grid_spec=pltpu.PrefetchScalarGridSpec(
                num_scalar_prefetch=1,
                grid=(pairs,),
                in_specs=[whole(p.shape) for p in parts[half]]
                + [whole(wd.shape)]
                + [pl.BlockSpec(memory_space=pl.ANY)] * len(earlier),
                out_specs=[
                    per_sample((cells, 3 * co)),
                    pl.BlockSpec((1, ci, cells), place_of),
                    per_sample((ci, cells)),
                ],
            ),
            out_shape=[
                pltpu.HBM((pairs, cells, 3 * co), BF16),
                pltpu.HBM((batch, ci, cells), F32),
                pltpu.HBM((pairs, ci, cells), F32),
            ],
            input_output_aliases={SIDE + 2: 1} if earlier else {},
            compiler_params=params,
            name="dgrad",
        )(place, *parts[half], wd, *earlier)
        return pltpu.with_memory_space_constraint(taps, pltpu.HBM), terms, swap_cores(other)

    taps_a, terms, term_a = dgrad(0, [])
    taps_b, terms, term_b = dgrad(1, [terms])
    samples = [taken(gathered, (1 - core) * 2 + half, pairs, 0) for half in range(2)]
    samples, term_a, term_b = lax.optimization_barrier((samples, term_a, term_b))
    samples = [swap_cores(sample) for sample in samples]
    terms = lax.dynamic_update_slice_in_dim(terms, term_a, (1 - core) * mine, 0)
    terms = lax.dynamic_update_slice_in_dim(terms, term_b, (1 - core) * mine + pairs, 0)
    grad_input = lax.psum_scatter(terms, "cout", scatter_dimension=0, tiled=True).astype(BF16)

    rows = SIDE * co + NOTE
    sent = jax.ShapeDtypeStruct((SIDE - 1, pairs, rows, PLANE), F32)
    kept = jax.ShapeDtypeStruct((pairs, rows, PLANE), F32)

    def forward(half):
        columns, msg, own = pl.pallas_call(
            functools.partial(fwd_kernel, half),
            grid_spec=pltpu.PrefetchScalarGridSpec(
                num_scalar_prefetch=1,
                grid=(pairs,),
                in_specs=[
                    pl.BlockSpec((1, ci, cells), lambda n, place: (place[2] * mine + half * pairs + n, 0, 0)),
                    per_sample((ci, cells)),
                    whole(wa.shape),
                ],
                out_specs=[pl.BlockSpec(memory_space=pltpu.VMEM), whole(sent.shape), whole(kept.shape)],
                scratch_shapes=[pltpu.VMEM((SX + 2, 3 * co, PLANE), F32), pltpu.VMEM((SX, co, PLANE), F32)],
            ),
            out_shape=[pltpu.VMEM((pairs, 9 * 2 * ci, cells), BF16), sent, kept],
            compiler_params=params,
            name="forward",
        )(place, gathered, samples[half], wa)
        return columns, msg, own

    columns_a, msg_a, own_a = forward(0)
    columns_b, msg_b, own_b = forward(1)

    def reduce_stage(msg, moves):
        return [move(msg[i].astype(F16)).astype(F32) for i, move in enumerate(moves)]

    rows = co + NOTE
    sent = jax.ShapeDtypeStruct((SIDE - 1, pairs, rows, PLANE), F32)
    kept = jax.ShapeDtypeStruct((pairs, rows, PLANE), F32)

    def turn(own, msg, moves):
        return pl.pallas_call(turn_kernel, out_shape=[sent, kept], compiler_params=params, name="turn")(
            own, *reduce_stage(msg, moves)
        )

    msg_a, own_a = turn(own_a, msg_a, along_x)
    ends_a = [own_a, *reduce_stage(msg_a, along_y)]
    msg_b, own_b = turn(own_b, msg_b, along_y)
    ends_b = [own_b, *reduce_stage(msg_b, along_x)]
    ends = ends_a + ends_b
    own, other = pl.pallas_call(
        wgrad_kernel,
        grid_spec=pltpu.PrefetchScalarGridSpec(
            num_scalar_prefetch=1,
            grid=(pairs,),
            in_specs=[pl.BlockSpec(memory_space=pltpu.VMEM)] * 2 + [per_sample((cells, 3 * co))] * 2,
            out_specs=[whole((27, ci, co))] * 2,
            scratch_shapes=[pltpu.VMEM((9 * 2 * ci, 3 * co), F32)],
        ),
        out_shape=[jax.ShapeDtypeStruct((27, ci, co), F32)] * 2,
        compiler_params=params,
        name="wgrad",
    )(place, columns_a, columns_b, taps_a, taps_b)
    grad_weight = (own + swap_cores(other)) / math.sqrt(batch * cells)
    ends, grad_weight = lax.optimization_barrier((ends, grad_weight))
    own, other = pl.pallas_call(
        last_kernel,
        grid_spec=pltpu.PrefetchScalarGridSpec(
            num_scalar_prefetch=1,
            grid=(1,),
            in_specs=[whole(e.shape) for e in ends],
            out_specs=[whole((mine, PLANE // 2, co))] * 2,
        ),
        out_shape=[jax.ShapeDtypeStruct((mine, PLANE // 2, co), BF16)] * 2,
        compiler_params=params,
        name="last",
    )(place, *ends)
    output = jnp.transpose(in_order(own, swap_cores(other), 0), (0, 2, 1))
    return output, grad_input, grad_weight


def solution(mesh):
    placed = (P("cout", "cin", None), P(None, "cin", "cout"), P(None, "cout", "cin"))
    return jax.shard_map(
        body,
        mesh=mesh,
        in_specs=placed,
        out_specs=(P(None, "cout", "cin"), P("cout", "cin", None), P(None, "cin", "cout")),
        check_vma=False,
    )
```

```python
import functools
import math

import jax
import jax.numpy as jnp
from jax import lax
from jax.experimental import pallas as pl
from jax.experimental.pallas import tpu as pltpu
from jax.sharding import PartitionSpec as P

SX = 16
SY = 16
SZ = 8
PLANE = SY * SZ
SIDE = 4
BF16 = jnp.bfloat16
F16 = jnp.float16
F32 = jnp.float32

in_plane = [(b, c) for b in (-1, 0, 1) for c in (-1, 0, 1)]
VMEM_LIMIT = 24 * 1024 * 1024
NOTE = 16
CHUNKS = 2
TINY = 1e-32


def move_xy(value, dy, dx, flip=0):
    pairs = []
    for y in range(SIDE):
        for x in range(SIDE):
            for core in range(2):
                target = ((y + dy) % SIDE * SIDE + (x + dx) % SIDE) * 2 + (core ^ flip)
                pairs.append(((y * SIDE + x) * 2 + core, target))
    return lax.ppermute(value, "cin", pairs)


def swap_cores(value):
    return move_xy(value, 0, 0, 1)


def plane_mask(rows, b, c):
    lane = lax.broadcasted_iota(jnp.int32, (rows, PLANE), 1)
    y = (lane >> 3) + b
    z = (lane & 7) + c
    return (y >= 0) & (y < SY) & (z >= 0) & (z < SZ)


def dgrad_kernel(half, place, *refs):
    parts, wd_ref = refs[:SIDE], refs[SIDE]
    taps_ref, own_ref, other_ref = refs[-3:]
    ci = own_ref.shape[1]
    co = taps_ref.shape[2] // 3
    n = pl.program_id(0)
    my_y, my_x, core = place[0], place[1], place[2]

    def fill(y_first):
        for first in range(SIDE):
            for second in range(SIDE):
                step_y, step_x = (first, second) if y_first else (second, first)
                y = lax.rem(my_y - step_y + SIDE, SIDE)
                x = lax.rem(my_x - step_x + SIDE, SIDE)
                p = y * SIDE + x
                cells = parts[first][second, n]

                def put(q, column):
                    row = pl.multiple_of(q * PLANE, PLANE)
                    taps_ref[0, pl.ds(row, PLANE), column * co : (column + 1) * co] = cells

                put(p, 1)
                pl.when(p > 0)(lambda: put(p - 1, 0))
                pl.when(p < SX - 1)(lambda: put(p + 1, 2))

    taps_ref[0, (SX - 1) * PLANE :, 0:co] = jnp.zeros((PLANE, co), BF16)
    taps_ref[0, 0:PLANE, 2 * co :] = jnp.zeros((PLANE, co), BF16)
    fill(half == 0)

    wd = wd_ref[...]
    masks = [plane_mask(2 * ci, -b, -c) for b, c in in_plane]
    step = 4
    for first in range(0, SX, step):
        rows = taps_ref[0, first * PLANE : (first + step) * PLANE, :]
        product = lax.dot_general(wd, rows, (((1,), (1,)), ((), ())), preferred_element_type=F32)
        for j in range(step):
            total = None
            for index, (b, c) in enumerate(in_plane):
                term = product[index * 2 * ci : (index + 1) * 2 * ci, j * PLANE : (j + 1) * PLANE]
                shift = (b * SZ + c) % PLANE
                if shift:
                    term = jnp.where(masks[index], pltpu.roll(term, shift, 1), 0.0)
                total = term if total is None else total + term
            lanes = slice((first + j) * PLANE, (first + j + 1) * PLANE)
            low, high = total[:ci], total[ci:]
            own_ref[0, :, lanes] = jnp.where(core == 0, low, high)
            other_ref[0, :, lanes] = jnp.where(core == 0, high, low)


def fwd_kernel(half, place, own_ref, other_ref, wa_ref, cols_ref, msg, own, stage, sums):
    ci = own_ref.shape[1]
    co = wa_ref.shape[0] // 3
    n = pl.program_id(0)
    my_y, my_x, core = place[0], place[1], place[2]
    masks = [plane_mask(2 * ci, b, c) for b, c in in_plane]

    @pl.when(n == 0)
    def _():
        stage[0] = jnp.zeros(stage.shape[1:], F32)
        stage[SX + 1] = jnp.zeros(stage.shape[1:], F32)

    for p in range(SX):
        lanes = slice(p * PLANE, (p + 1) * PLANE)
        mine = own_ref[0, :, lanes].astype(F32)
        got = other_ref[0, :, lanes].astype(F32)
        cells = jnp.concatenate([jnp.where(core == 0, mine, got), jnp.where(core == 0, got, mine)], axis=0)
        for index, (b, c) in enumerate(in_plane):
            shift = -(b * SZ + c) % PLANE
            term = cells
            if shift:
                term = jnp.where(masks[index], pltpu.roll(term, shift, 1), 0.0)
            cols_ref[n, index * 2 * ci : (index + 1) * 2 * ci, lanes] = term.astype(BF16)

    step = 4
    for first in range(0, SX, step):
        lanes = slice(first * PLANE, (first + step) * PLANE)
        product = jnp.dot(wa_ref[...], cols_ref[n, :, lanes], preferred_element_type=F32)
        for j in range(step):
            stage[first + j + 1] = product[:, j * PLANE : (j + 1) * PLANE]

    peak = jnp.zeros((co, PLANE), F32)
    for p in range(SX):
        total = stage[p, 0:co] + stage[p + 1, co : 2 * co] + stage[p + 2, 2 * co :]
        sums[p] = total
        peak = jnp.maximum(peak, jnp.abs(total))
    peak = jnp.full((NOTE, PLANE), jnp.maximum(jnp.max(peak), TINY), F32)
    power = 14.0 - jnp.ceil(jnp.log2(peak))
    factor = jnp.exp2(power[0:1])
    rows = SIDE * co

    def send(y_first):
        for first in range(SIDE):
            if first == 0:
                own[n, rows:] = power
            else:
                msg[first - 1, n, rows:] = power
            for second in range(SIDE):
                step_y, step_x = (first, second) if y_first else (second, first)
                y = lax.rem(my_y + step_y, SIDE)
                x = lax.rem(my_x + step_x, SIDE)
                total = sums[y * SIDE + x]
                if first == 0:
                    own[n, second * co : (second + 1) * co] = total
                else:
                    msg[first - 1, n, second * co : (second + 1) * co] = total * factor

    send(half == 1)


def arrived(own, messages, rows):
    total, least = own[:, :rows], own[:, rows:]
    for message in messages:
        power = message[:, rows:]
        total = total + message[:, :rows] * jnp.exp2(-power[:, 0:1])
        least = jnp.minimum(least, power)
    return total, least


def turn_kernel(own, one, two, three, msg, mine):
    rows = own.shape[1] - NOTE
    size = rows // SIDE
    total, least = arrived(own[...], [one[...], two[...], three[...]], rows)
    power = least - 2.0
    mine[:, :size] = total[:, :size]
    mine[:, size:] = power
    for step in range(1, SIDE):
        msg[step - 1, :, :size] = total[:, step * size : (step + 1) * size] * jnp.exp2(power[:, 0:1])
        msg[step - 1, :, size:] = power


def last_kernel(place, *refs):
    ins, own_ref, other_ref = refs[:8], refs[8], refs[9]
    part = PLANE // 2
    for half in range(2):
        own, messages = ins[4 * half], ins[4 * half + 1 : 4 * half + 4]
        rows = own.shape[1] - NOTE
        total, _ = arrived(own[...], [m[...] for m in messages], rows)
        for at in range(total.shape[0]):
            cells = total[at].T.astype(BF16)
            low, high = cells[:part], cells[part:]
            own_ref[half * total.shape[0] + at] = jnp.where(place[2] == 0, low, high)
            other_ref[half * total.shape[0] + at] = jnp.where(place[2] == 0, high, low)


def wgrad_kernel(place, cols_a, cols_b, taps_a, taps_b, own_ref, other_ref, acc):
    ci, co = own_ref.shape[1:]
    n, k = pl.program_id(0), pl.program_id(1)
    depth = taps_a.shape[1]
    lanes = pl.ds(pl.multiple_of(k * depth, depth), depth)

    @pl.when((n == 0) & (k == 0))
    def _():
        acc[...] = jnp.zeros_like(acc)

    acc[...] += jnp.dot(cols_a[n, :, lanes], taps_a[0], preferred_element_type=F32)
    acc[...] += jnp.dot(cols_b[n, :, lanes], taps_b[0], preferred_element_type=F32)

    @pl.when((n == pl.num_programs(0) - 1) & (k == pl.num_programs(1) - 1))
    def _():
        for tap in range(27):
            first, column = tap % 9 * 2 * ci, tap // 9 * co
            low = acc[first : first + ci, column : column + co]
            high = acc[first + ci : first + 2 * ci, column : column + co]
            own_ref[tap] = jnp.where(place[2] == 0, low, high)
            other_ref[tap] = jnp.where(place[2] == 0, high, low)


def place_kernel(place, _, term_a, term_b, terms, sems):
    pairs = term_a.shape[0]
    first = (1 - place[2]) * 2 * pairs
    copies = [
        pltpu.make_async_copy(term, terms.at[pl.ds(first + half * pairs, pairs)], sems.at[half])
        for half, term in enumerate((term_a, term_b))
    ]
    for copy in copies:
        copy.start()
    for copy in copies:
        copy.wait()


def whole(shape):
    return pl.BlockSpec(memory_space=pltpu.VMEM)


def per_sample(shape):
    return pl.BlockSpec((1,) + shape, lambda n, *_: (n,) + (0,) * len(shape))


def body(inputs, weight, grad_out):
    ci, co = weight.shape[1], weight.shape[2]
    where_cin = lax.axis_index("cin")
    core = where_cin % 2
    place = jnp.stack([where_cin // 2 // SIDE, where_cin // 2 % SIDE, core]).astype(jnp.int32)
    batch = grad_out.shape[0]
    mine = batch // 2
    pairs = mine // 2
    first_core = core == 0

    def taken(value, which, size, axis):
        return lax.dynamic_slice_in_dim(value, which * size, size, axis)

    def in_order(own, other, axis):
        return jnp.where(
            first_core,
            jnp.concatenate([own, other], axis),
            jnp.concatenate([other, own], axis),
        )

    gathered = lax.all_gather(inputs, "cout", axis=0, tiled=True)

    cotangent = jnp.transpose(grad_out, (0, 2, 1))
    got = swap_cores(taken(cotangent, 1 - core, mine, 0))
    plane = in_order(taken(cotangent, core, mine, 0), got, 1)
    along_x = [functools.partial(move_xy, dy=0, dx=s) for s in (1, 2, 3)]
    along_y = [functools.partial(move_xy, dy=s, dx=0) for s in (1, 2, 3)]

    def gather_stage(value, moves):
        return [value] + [move(value) for move in moves]

    near_a, near_b = lax.optimization_barrier(
        (gather_stage(plane[:pairs], along_x), gather_stage(plane[pairs:], along_y))
    )
    row_a, row_b = lax.optimization_barrier((jnp.stack(near_a), jnp.stack(near_b)))
    parts = gather_stage(row_a, along_y), gather_stage(row_b, along_x)

    pair = in_order(weight, swap_cores(weight), 1)
    wd = jnp.transpose(pair.reshape(3, 9, 2 * ci, co), (1, 2, 0, 3)).reshape(9 * 2 * ci, 3 * co)
    wa = wd.T

    cells = inputs.shape[2]
    params = pltpu.CompilerParams(vmem_limit_bytes=VMEM_LIMIT)
    def dgrad(half, earlier):
        place_of = lambda n, place: (place[2] * mine + half * pairs + n, 0, 0)
        taps, terms, other = pl.pallas_call(
            functools.partial(dgrad_kernel, half),
            grid_spec=pltpu.PrefetchScalarGridSpec(
                num_scalar_prefetch=1,
                grid=(pairs,),
                in_specs=[whole(p.shape) for p in parts[half]]
                + [whole(wd.shape)]
                + [pl.BlockSpec(memory_space=pl.ANY)] * len(earlier),
                out_specs=[
                    per_sample((cells, 3 * co)),
                    pl.BlockSpec((1, ci, cells), place_of),
                    per_sample((ci, cells)),
                ],
            ),
            out_shape=[
                pltpu.HBM((pairs, cells, 3 * co), BF16),
                pltpu.HBM((batch, ci, cells), F32),
                pltpu.HBM((pairs, ci, cells), F32),
            ],
            input_output_aliases={SIDE + 2: 1} if earlier else {},
            compiler_params=params,
            name="dgrad",
        )(place, *parts[half], wd, *earlier)
        return pltpu.with_memory_space_constraint(taps, pltpu.HBM), terms, swap_cores(other)

    taps_a, terms, term_a = dgrad(0, [])
    taps_b, terms, term_b = dgrad(1, [terms])
    samples = [taken(gathered, (1 - core) * 2 + half, pairs, 0) for half in range(2)]
    samples, term_a, term_b = lax.optimization_barrier((samples, term_a, term_b))
    samples = [swap_cores(sample) for sample in samples]
    terms = pl.pallas_call(
        place_kernel,
        grid_spec=pltpu.PrefetchScalarGridSpec(
            num_scalar_prefetch=1,
            grid=(1,),
            in_specs=[pl.BlockSpec(memory_space=pl.ANY)] * 3,
            out_specs=pl.BlockSpec(memory_space=pl.ANY),
            scratch_shapes=[pltpu.SemaphoreType.DMA((2,))],
        ),
        out_shape=pltpu.HBM(terms.shape, F32),
        input_output_aliases={1: 0},
        compiler_params=params,
        name="place",
    )(place, terms, term_a, term_b)
    grad_input = lax.psum_scatter(terms, "cout", scatter_dimension=0, tiled=True).astype(BF16)

    rows = SIDE * co + NOTE
    sent = jax.ShapeDtypeStruct((SIDE - 1, pairs, rows, PLANE), F32)
    kept = jax.ShapeDtypeStruct((pairs, rows, PLANE), F32)

    def forward(half):
        columns, msg, own = pl.pallas_call(
            functools.partial(fwd_kernel, half),
            grid_spec=pltpu.PrefetchScalarGridSpec(
                num_scalar_prefetch=1,
                grid=(pairs,),
                in_specs=[
                    pl.BlockSpec((1, ci, cells), lambda n, place: (place[2] * mine + half * pairs + n, 0, 0)),
                    per_sample((ci, cells)),
                    whole(wa.shape),
                ],
                out_specs=[pl.BlockSpec(memory_space=pltpu.VMEM), whole(sent.shape), whole(kept.shape)],
                scratch_shapes=[pltpu.VMEM((SX + 2, 3 * co, PLANE), F32), pltpu.VMEM((SX, co, PLANE), F32)],
            ),
            out_shape=[pltpu.VMEM((pairs, 9 * 2 * ci, cells), BF16), sent, kept],
            compiler_params=params,
            name="forward",
        )(place, gathered, samples[half], wa)
        return columns, msg, own

    columns_a, msg_a, own_a = forward(0)
    columns_b, msg_b, own_b = forward(1)

    def reduce_stage(msg, moves):
        return [move(msg[i].astype(F16)).astype(F32) for i, move in enumerate(moves)]

    rows = co + NOTE
    sent = jax.ShapeDtypeStruct((SIDE - 1, pairs, rows, PLANE), F32)
    kept = jax.ShapeDtypeStruct((pairs, rows, PLANE), F32)

    def turn(own, msg, moves):
        return pl.pallas_call(turn_kernel, out_shape=[sent, kept], compiler_params=params, name="turn")(
            own, *reduce_stage(msg, moves)
        )

    msg_a, own_a = turn(own_a, msg_a, along_x)
    ends_a = [own_a, *reduce_stage(msg_a, along_y)]
    msg_b, own_b = turn(own_b, msg_b, along_y)
    ends_b = [own_b, *reduce_stage(msg_b, along_x)]
    ends = ends_a + ends_b
    own, other = pl.pallas_call(
        wgrad_kernel,
        grid_spec=pltpu.PrefetchScalarGridSpec(
            num_scalar_prefetch=1,
            grid=(pairs, CHUNKS),
            in_specs=[pl.BlockSpec(memory_space=pltpu.VMEM)] * 2
            + [pl.BlockSpec((1, cells // CHUNKS, 3 * co), lambda n, k, *_: (n, k, 0))] * 2,
            out_specs=[whole((27, ci, co))] * 2,
            scratch_shapes=[pltpu.VMEM((9 * 2 * ci, 3 * co), F32)],
        ),
        out_shape=[jax.ShapeDtypeStruct((27, ci, co), F32)] * 2,
        compiler_params=params,
        name="wgrad",
    )(place, columns_a, columns_b, taps_a, taps_b)
    grad_weight = (own + swap_cores(other)) / math.sqrt(batch * cells)
    ends, grad_weight = lax.optimization_barrier((ends, grad_weight))
    own, other = pl.pallas_call(
        last_kernel,
        grid_spec=pltpu.PrefetchScalarGridSpec(
            num_scalar_prefetch=1,
            grid=(1,),
            in_specs=[whole(e.shape) for e in ends],
            out_specs=[whole((mine, PLANE // 2, co))] * 2,
        ),
        out_shape=[jax.ShapeDtypeStruct((mine, PLANE // 2, co), BF16)] * 2,
        compiler_params=params,
        name="last",
    )(place, *ends)
    got, grad_input = lax.optimization_barrier((swap_cores(other), grad_input))
    output = jnp.transpose(in_order(own, got, 0), (0, 2, 1))
    return output, grad_input, grad_weight


def solution(mesh):
    placed = (P("cout", "cin", None), P(None, "cin", "cout"), P(None, "cout", "cin"))
    return jax.shard_map(
        body,
        mesh=mesh,
        in_specs=placed,
        out_specs=(P(None, "cout", "cin"), P("cout", "cin", None), P(None, "cin", "cout")),
        check_vma=False,
    )
```

```python
import functools
import math

import jax
import jax.numpy as jnp
from jax import lax
from jax.experimental import pallas as pl
from jax.experimental.pallas import tpu as pltpu
from jax.sharding import PartitionSpec as P

SX = 16
SY = 16
SZ = 8
PLANE = SY * SZ
SIDE = 4
BF16 = jnp.bfloat16
F16 = jnp.float16
F32 = jnp.float32

in_plane = [(b, c) for b in (-1, 0, 1) for c in (-1, 0, 1)]
VMEM_LIMIT = 24 * 1024 * 1024
NOTE = 16
CHUNKS = 2
TINY = 1e-32


def move_xy(value, dy, dx, flip=0):
    pairs = []
    for y in range(SIDE):
        for x in range(SIDE):
            for core in range(2):
                target = ((y + dy) % SIDE * SIDE + (x + dx) % SIDE) * 2 + (core ^ flip)
                pairs.append(((y * SIDE + x) * 2 + core, target))
    return lax.ppermute(value, "cin", pairs)


def swap_cores(value):
    return move_xy(value, 0, 0, 1)


def plane_mask(rows, b, c):
    lane = lax.broadcasted_iota(jnp.int32, (rows, PLANE), 1)
    y = (lane >> 3) + b
    z = (lane & 7) + c
    return (y >= 0) & (y < SY) & (z >= 0) & (z < SZ)


def dgrad_kernel(half, place, *refs):
    parts, wd_ref = refs[:SIDE], refs[SIDE]
    taps_ref, own_ref, other_ref = refs[-3:]
    ci = own_ref.shape[1]
    co = taps_ref.shape[2] // 3
    n = pl.program_id(0)
    my_y, my_x, core = place[0], place[1], place[2]

    def fill(y_first):
        for first in range(SIDE):
            for second in range(SIDE):
                step_y, step_x = (first, second) if y_first else (second, first)
                y = lax.rem(my_y - step_y + SIDE, SIDE)
                x = lax.rem(my_x - step_x + SIDE, SIDE)
                p = y * SIDE + x
                cells = parts[first][second, n]

                def put(q, column):
                    row = pl.multiple_of(q * PLANE, PLANE)
                    taps_ref[0, pl.ds(row, PLANE), column * co : (column + 1) * co] = cells

                put(p, 1)
                pl.when(p > 0)(lambda: put(p - 1, 0))
                pl.when(p < SX - 1)(lambda: put(p + 1, 2))

    taps_ref[0, (SX - 1) * PLANE :, 0:co] = jnp.zeros((PLANE, co), BF16)
    taps_ref[0, 0:PLANE, 2 * co :] = jnp.zeros((PLANE, co), BF16)
    fill(half == 0)

    wd = wd_ref[...]
    masks = [plane_mask(2 * ci, -b, -c) for b, c in in_plane]
    step = 4
    for first in range(0, SX, step):
        rows = taps_ref[0, first * PLANE : (first + step) * PLANE, :]
        product = lax.dot_general(wd, rows, (((1,), (1,)), ((), ())), preferred_element_type=F32)
        for j in range(step):
            total = None
            for index, (b, c) in enumerate(in_plane):
                term = product[index * 2 * ci : (index + 1) * 2 * ci, j * PLANE : (j + 1) * PLANE]
                shift = (b * SZ + c) % PLANE
                if shift:
                    term = jnp.where(masks[index], pltpu.roll(term, shift, 1), 0.0)
                total = term if total is None else total + term
            lanes = slice((first + j) * PLANE, (first + j + 1) * PLANE)
            low, high = total[:ci], total[ci:]
            own_ref[0, :, lanes] = jnp.where(core == 0, low, high)
            other_ref[0, :, lanes] = jnp.where(core == 0, high, low)


def fwd_kernel(half, place, own_ref, other_ref, wa_ref, cols_ref, msg, own, stage, sums):
    ci = own_ref.shape[1]
    co = wa_ref.shape[0] // 3
    n = pl.program_id(0)
    my_y, my_x, core = place[0], place[1], place[2]
    masks = [plane_mask(2 * ci, b, c) for b, c in in_plane]

    @pl.when(n == 0)
    def _():
        stage[0] = jnp.zeros(stage.shape[1:], F32)
        stage[SX + 1] = jnp.zeros(stage.shape[1:], F32)

    for p in range(SX):
        lanes = slice(p * PLANE, (p + 1) * PLANE)
        mine = own_ref[0, :, lanes].astype(F32)
        got = other_ref[0, :, lanes].astype(F32)
        cells = jnp.concatenate([jnp.where(core == 0, mine, got), jnp.where(core == 0, got, mine)], axis=0)
        for index, (b, c) in enumerate(in_plane):
            shift = -(b * SZ + c) % PLANE
            term = cells
            if shift:
                term = jnp.where(masks[index], pltpu.roll(term, shift, 1), 0.0)
            cols_ref[n, index * 2 * ci : (index + 1) * 2 * ci, lanes] = term.astype(BF16)

    step = 4
    for first in range(0, SX, step):
        lanes = slice(first * PLANE, (first + step) * PLANE)
        product = jnp.dot(wa_ref[...], cols_ref[n, :, lanes], preferred_element_type=F32)
        for j in range(step):
            stage[first + j + 1] = product[:, j * PLANE : (j + 1) * PLANE]

    peak = jnp.zeros((co, PLANE), F32)
    for p in range(SX):
        total = stage[p, 0:co] + stage[p + 1, co : 2 * co] + stage[p + 2, 2 * co :]
        sums[p] = total
        peak = jnp.maximum(peak, jnp.abs(total))
    peak = jnp.full((NOTE, PLANE), jnp.maximum(jnp.max(peak), TINY), F32)
    power = 14.0 - jnp.ceil(jnp.log2(peak))
    factor = jnp.exp2(power[0:1])
    rows = SIDE * co

    def send(y_first):
        for first in range(SIDE):
            if first == 0:
                own[n, rows:] = power
            else:
                msg[first - 1, n, rows:] = power
            for second in range(SIDE):
                step_y, step_x = (first, second) if y_first else (second, first)
                y = lax.rem(my_y + step_y, SIDE)
                x = lax.rem(my_x + step_x, SIDE)
                total = sums[y * SIDE + x]
                if first == 0:
                    own[n, second * co : (second + 1) * co] = total
                else:
                    msg[first - 1, n, second * co : (second + 1) * co] = total * factor

    send(half == 1)


def arrived(own, messages, rows):
    total, least = own[:, :rows], own[:, rows:]
    for message in messages:
        power = message[:, rows:]
        total = total + message[:, :rows] * jnp.exp2(-power[:, 0:1])
        least = jnp.minimum(least, power)
    return total, least


def turn_kernel(own, one, two, three, msg, mine):
    rows = own.shape[1] - NOTE
    size = rows // SIDE
    total, least = arrived(own[...], [one[...], two[...], three[...]], rows)
    power = least - 2.0
    mine[:, :size] = total[:, :size]
    mine[:, size:] = power
    for step in range(1, SIDE):
        msg[step - 1, :, :size] = total[:, step * size : (step + 1) * size] * jnp.exp2(power[:, 0:1])
        msg[step - 1, :, size:] = power


def last_kernel(scale, place, *refs):
    ins, sum_ref, got_ref, own_ref, other_ref, weight_ref = refs[:8], *refs[8:]
    weight_ref[...] = (sum_ref[...] + got_ref[...]) * scale
    part = PLANE // 2
    for half in range(2):
        own, messages = ins[4 * half], ins[4 * half + 1 : 4 * half + 4]
        rows = own.shape[1] - NOTE
        total, _ = arrived(own[...], [m[...] for m in messages], rows)
        for at in range(total.shape[0]):
            cells = total[at].T.astype(BF16)
            low, high = cells[:part], cells[part:]
            own_ref[half * total.shape[0] + at] = jnp.where(place[2] == 0, low, high)
            other_ref[half * total.shape[0] + at] = jnp.where(place[2] == 0, high, low)


def wgrad_kernel(place, cols_a, cols_b, taps_a, taps_b, own_ref, other_ref, acc):
    ci, co = own_ref.shape[1:]
    n, k = pl.program_id(0), pl.program_id(1)
    depth = taps_a.shape[1]
    lanes = pl.ds(pl.multiple_of(k * depth, depth), depth)

    @pl.when((n == 0) & (k == 0))
    def _():
        acc[...] = jnp.zeros_like(acc)

    acc[...] += jnp.dot(cols_a[n, :, lanes], taps_a[0], preferred_element_type=F32)
    acc[...] += jnp.dot(cols_b[n, :, lanes], taps_b[0], preferred_element_type=F32)

    @pl.when((n == pl.num_programs(0) - 1) & (k == pl.num_programs(1) - 1))
    def _():
        for tap in range(27):
            first, column = tap % 9 * 2 * ci, tap // 9 * co
            low = acc[first : first + ci, column : column + co]
            high = acc[first + ci : first + 2 * ci, column : column + co]
            own_ref[tap] = jnp.where(place[2] == 0, low, high)
            other_ref[tap] = jnp.where(place[2] == 0, high, low)


def place_kernel(place, _, term_a, term_b, terms, sems):
    pairs = term_a.shape[0]
    first = (1 - place[2]) * 2 * pairs
    copies = [
        pltpu.make_async_copy(term, terms.at[pl.ds(first + half * pairs, pairs)], sems.at[half])
        for half, term in enumerate((term_a, term_b))
    ]
    for copy in copies:
        copy.start()
    for copy in copies:
        copy.wait()


def whole(shape):
    return pl.BlockSpec(memory_space=pltpu.VMEM)


def per_sample(shape):
    return pl.BlockSpec((1,) + shape, lambda n, *_: (n,) + (0,) * len(shape))


def body(inputs, weight, grad_out):
    ci, co = weight.shape[1], weight.shape[2]
    where_cin = lax.axis_index("cin")
    core = where_cin % 2
    place = jnp.stack([where_cin // 2 // SIDE, where_cin // 2 % SIDE, core]).astype(jnp.int32)
    batch = grad_out.shape[0]
    mine = batch // 2
    pairs = mine // 2
    first_core = core == 0

    def taken(value, which, size, axis):
        return lax.dynamic_slice_in_dim(value, which * size, size, axis)

    def in_order(own, other, axis):
        return jnp.where(
            first_core,
            jnp.concatenate([own, other], axis),
            jnp.concatenate([other, own], axis),
        )

    gathered = lax.all_gather(inputs, "cout", axis=0, tiled=True)

    cotangent = jnp.transpose(grad_out, (0, 2, 1))
    got = swap_cores(taken(cotangent, 1 - core, mine, 0))
    plane = in_order(taken(cotangent, core, mine, 0), got, 1)
    along_x = [functools.partial(move_xy, dy=0, dx=s) for s in (1, 2, 3)]
    along_y = [functools.partial(move_xy, dy=s, dx=0) for s in (1, 2, 3)]

    def gather_stage(value, moves):
        return [value] + [move(value) for move in moves]

    near_a, near_b = lax.optimization_barrier(
        (gather_stage(plane[:pairs], along_x), gather_stage(plane[pairs:], along_y))
    )
    row_a, row_b = lax.optimization_barrier((jnp.stack(near_a), jnp.stack(near_b)))
    parts = gather_stage(row_a, along_y), gather_stage(row_b, along_x)

    pair = in_order(weight, swap_cores(weight), 1)
    wd = jnp.transpose(pair.reshape(3, 9, 2 * ci, co), (1, 2, 0, 3)).reshape(9 * 2 * ci, 3 * co)
    wa = wd.T

    cells = inputs.shape[2]
    params = pltpu.CompilerParams(vmem_limit_bytes=VMEM_LIMIT)
    def dgrad(half, earlier):
        place_of = lambda n, place: (place[2] * mine + half * pairs + n, 0, 0)
        taps, terms, other = pl.pallas_call(
            functools.partial(dgrad_kernel, half),
            grid_spec=pltpu.PrefetchScalarGridSpec(
                num_scalar_prefetch=1,
                grid=(pairs,),
                in_specs=[whole(p.shape) for p in parts[half]]
                + [whole(wd.shape)]
                + [pl.BlockSpec(memory_space=pl.ANY)] * len(earlier),
                out_specs=[
                    per_sample((cells, 3 * co)),
                    pl.BlockSpec((1, ci, cells), place_of),
                    per_sample((ci, cells)),
                ],
            ),
            out_shape=[
                pltpu.HBM((pairs, cells, 3 * co), BF16),
                pltpu.HBM((batch, ci, cells), F32),
                pltpu.HBM((pairs, ci, cells), F32),
            ],
            input_output_aliases={SIDE + 2: 1} if earlier else {},
            compiler_params=params,
            name="dgrad",
        )(place, *parts[half], wd, *earlier)
        return pltpu.with_memory_space_constraint(taps, pltpu.HBM), terms, swap_cores(other)

    taps_a, terms, term_a = dgrad(0, [])
    taps_b, terms, term_b = dgrad(1, [terms])
    samples = [taken(gathered, (1 - core) * 2 + half, pairs, 0) for half in range(2)]
    samples, term_a, term_b = lax.optimization_barrier((samples, term_a, term_b))
    samples = [swap_cores(sample) for sample in samples]
    terms = pl.pallas_call(
        place_kernel,
        grid_spec=pltpu.PrefetchScalarGridSpec(
            num_scalar_prefetch=1,
            grid=(1,),
            in_specs=[pl.BlockSpec(memory_space=pl.ANY)] * 3,
            out_specs=pl.BlockSpec(memory_space=pl.ANY),
            scratch_shapes=[pltpu.SemaphoreType.DMA((2,))],
        ),
        out_shape=pltpu.HBM(terms.shape, F32),
        input_output_aliases={1: 0},
        compiler_params=params,
        name="place",
    )(place, terms, term_a, term_b)
    grad_input = lax.psum_scatter(terms, "cout", scatter_dimension=0, tiled=True).astype(BF16)

    rows = SIDE * co + NOTE
    sent = jax.ShapeDtypeStruct((SIDE - 1, pairs, rows, PLANE), F32)
    kept = jax.ShapeDtypeStruct((pairs, rows, PLANE), F32)

    def forward(half):
        columns, msg, own = pl.pallas_call(
            functools.partial(fwd_kernel, half),
            grid_spec=pltpu.PrefetchScalarGridSpec(
                num_scalar_prefetch=1,
                grid=(pairs,),
                in_specs=[
                    pl.BlockSpec((1, ci, cells), lambda n, place: (place[2] * mine + half * pairs + n, 0, 0)),
                    per_sample((ci, cells)),
                    whole(wa.shape),
                ],
                out_specs=[pl.BlockSpec(memory_space=pltpu.VMEM), whole(sent.shape), whole(kept.shape)],
                scratch_shapes=[pltpu.VMEM((SX + 2, 3 * co, PLANE), F32), pltpu.VMEM((SX, co, PLANE), F32)],
            ),
            out_shape=[pltpu.VMEM((pairs, 9 * 2 * ci, cells), BF16), sent, kept],
            compiler_params=params,
            name="forward",
        )(place, gathered, samples[half], wa)
        return columns, msg, own

    columns_a, msg_a, own_a = forward(0)
    columns_b, msg_b, own_b = forward(1)

    def reduce_stage(msg, moves):
        return [move(msg[i].astype(F16)).astype(F32) for i, move in enumerate(moves)]

    rows = co + NOTE
    sent = jax.ShapeDtypeStruct((SIDE - 1, pairs, rows, PLANE), F32)
    kept = jax.ShapeDtypeStruct((pairs, rows, PLANE), F32)

    def turn(own, msg, moves):
        return pl.pallas_call(turn_kernel, out_shape=[sent, kept], compiler_params=params, name="turn")(
            own, *reduce_stage(msg, moves)
        )

    msg_a, own_a = turn(own_a, msg_a, along_x)
    ends_a = [own_a, *reduce_stage(msg_a, along_y)]
    msg_b, own_b = turn(own_b, msg_b, along_y)
    ends_b = [own_b, *reduce_stage(msg_b, along_x)]
    ends = ends_a + ends_b
    own, other = pl.pallas_call(
        wgrad_kernel,
        grid_spec=pltpu.PrefetchScalarGridSpec(
            num_scalar_prefetch=1,
            grid=(pairs, CHUNKS),
            in_specs=[pl.BlockSpec(memory_space=pltpu.VMEM)] * 2
            + [pl.BlockSpec((1, cells // CHUNKS, 3 * co), lambda n, k, *_: (n, k, 0))] * 2,
            out_specs=[whole((27, ci, co))] * 2,
            scratch_shapes=[pltpu.VMEM((9 * 2 * ci, 3 * co), F32)],
        ),
        out_shape=[jax.ShapeDtypeStruct((27, ci, co), F32)] * 2,
        compiler_params=params,
        name="wgrad",
    )(place, columns_a, columns_b, taps_a, taps_b)
    sums = [own, swap_cores(other)]
    own, other, grad_weight = pl.pallas_call(
        functools.partial(last_kernel, 1.0 / math.sqrt(batch * cells)),
        grid_spec=pltpu.PrefetchScalarGridSpec(
            num_scalar_prefetch=1,
            grid=(1,),
            in_specs=[whole(e.shape) for e in ends + sums],
            out_specs=[whole((mine, PLANE // 2, co))] * 2 + [pl.BlockSpec(own.shape, lambda *_: (0, 0, 0))],
        ),
        out_shape=[jax.ShapeDtypeStruct((mine, PLANE // 2, co), BF16)] * 2 + [jax.ShapeDtypeStruct(own.shape, F32)],
        compiler_params=params,
        name="last",
    )(place, *ends, *sums)
    got, grad_input = lax.optimization_barrier((swap_cores(other), grad_input))
    output = jnp.transpose(in_order(own, got, 0), (0, 2, 1))
    return output, grad_input, grad_weight


def solution(mesh):
    placed = (P("cout", "cin", None), P(None, "cin", "cout"), P(None, "cout", "cin"))
    return jax.shard_map(
        body,
        mesh=mesh,
        in_specs=placed,
        out_specs=(P(None, "cout", "cin"), P("cout", "cin", None), P(None, "cin", "cout")),
        check_vma=False,
    )
```
